256 devices in a mesh: prow: 32 (over x, z), pcol: 8 (over y, core).
Axes of the slice: x: 4, y: 4, z: 8, core: 2. Of those that a mesh axis runs over, the one named last changes fastest.
Arguments:
- matrix: bfloat16 [32, 3, 256, 8, 12, 256], P('prow', None, None, 'pcol')
- row_perm: int32 [32, 3, 256], P('prow'), may hold values from 0 to 255, as said below
- block_pattern: int32 [96, 96], replicated, may hold values from 0 to 1, as said below
Outputs:
- factored: bfloat16 [32, 3, 256, 8, 12, 256], P('prow', None, None, 'pcol')
The draws below stay inside these ranges and needn't reach their ends.
Inputs may be any that keep to these rules, and one draw needn't show every extreme that they name: `row_perm`: each row of 256 entries along the last dimension is a permutation of 0 to 255. `block_pattern`: 0 or 1. Diagonal blocks are 1 and block (1, 0) is 0. The pattern is closed under the fill of supernodes 0 and 1: if (i, k) and (k, j) are 1 with i > k and j > k, then (i, j) is 1 (for k = 1 after the fill of k = 0). For k = 0 and k = 1, the blocks (k, j) with j >= k that lie in one process-grid column (j % 8 fixed) hold at most 6 ones, and exactly 6 in some process-grid column.
All inputs are finite; a program needn't handle non-finite values.
Results may differ from the reference program's by a relative error of at most 0.0028.
Values may be sent and summed in bfloat16 or wider, within the bound.
No kernel may reach another device: no remote copies, remote signals or barrier semaphores. Data moves between devices by JAX's collectives and lax.ppermute only.
A program may use at most 128 MiB of HBM per device.

```python
import math
import jax
import jax.numpy as jnp
from jax import lax

B = 256
LR = 3
NEWTON = 3
NB = 96
LC = 12
UCAP = 6
N_PROW = 32
N_PCOL = 8


def shared_orders(key):
    row_keys = jax.random.split(key, NB)
    return jax.vmap(lambda row_key: jax.random.permutation(row_key, B))(row_keys)


def draw_row_perm(key, part):
    orders = shared_orders(key)
    return jnp.transpose(orders.reshape(LR, N_PROW, B), (1, 0, 2)).astype(jnp.int32)


def draw_matrix(key, part):
    orders = shared_orders(key)
    key = jax.random.fold_in(key, 11)
    noise_key, pivot_key = jax.random.split(key)
    log_low = math.log(8.0)
    log_high = math.log(24.0)
    block_ids = jnp.arange(NB)
    positions = jnp.arange(B)

    def draw_row(index):
        noise_values = jax.random.normal(jax.random.fold_in(noise_key, index), (B, NB, B), jnp.float32)
        noise_values = jnp.clip(noise_values, -6.0, 6.0)
        diagonal = (block_ids == index)[None, :, None]
        scaled = noise_values * jnp.where(diagonal, 0.1, 0.5)
        pivots = jnp.exp(jax.random.uniform(jax.random.fold_in(pivot_key, index), (B,), jnp.float32, log_low, log_high))
        row_order = lax.dynamic_index_in_dim(orders, index, 0, keepdims=False)
        placed = (row_order[None, :] == positions[:, None]).astype(jnp.float32) * pivots[None, :]
        return (scaled + jnp.where(diagonal, placed[:, None, :], 0.0)).astype(jnp.bfloat16)
    drawn_rows = lax.map(draw_row, block_ids)
    return jnp.transpose(drawn_rows.reshape(LR, N_PROW, B, LC, N_PCOL, B), (1, 0, 2, 4, 3, 5))


def draw_block_pattern(key, part):
    key = jax.random.fold_in(key, 23)
    base_key, column_key, row_key, heavy_key, count_key = jax.random.split(key, 5)
    row_index = jnp.arange(NB)[:, None]
    col_index = jnp.arange(NB)[None, :]
    pattern = jax.random.randint(base_key, (NB, NB), 0, 4) == 0
    column_draw = jax.random.randint(column_key, (NB, 2), 0, 2) == 1
    for supernode in range(2):
        pattern = pattern.at[:, supernode].set(column_draw[:, supernode] & (jnp.arange(NB) > supernode))
    local_cols = jnp.arange(LC)[:, None]
    grid_cols = jnp.arange(N_PCOL)[None, :]
    global_cols = local_cols * N_PCOL + grid_cols
    for supernode in range(2):
        valid_mask = global_cols >= supernode
        rank_draw = jax.random.randint(jax.random.fold_in(row_key, supernode), (LC, N_PCOL), 0, 1 << 20) * LC + local_cols
        scores = jnp.where(global_cols == supernode, -1, jnp.where(valid_mask, rank_draw, 1 << 30))
        positions = jnp.sum((scores[None, :, :] < scores[:, None, :]).astype(jnp.int32), axis=1)
        heavy_col = jax.random.randint(jax.random.fold_in(heavy_key, supernode), (), 0, N_PCOL)
        light_counts = jax.random.randint(jax.random.fold_in(count_key, supernode), (N_PCOL,), 1, max(1, UCAP // 2) + 1)
        counts = jnp.where(jnp.arange(N_PCOL) == heavy_col, UCAP, light_counts)
        chosen = (positions < counts[None, :]) & valid_mask
        pattern = pattern.at[supernode].set(chosen.reshape(NB))
    pattern = pattern | (row_index == col_index)
    for supernode in range(2):
        fill_in = pattern[:, supernode:supernode + 1] & pattern[supernode:supernode + 1, :]
        fill_in = fill_in & (row_index > supernode) & (col_index > supernode)
        pattern = pattern | fill_in
    return pattern.astype(jnp.int32)


def setup_inputs(seed: int = 0) -> dict:
    key_list = jax.random.split(jax.random.key(seed), 4)
    matrix = draw_matrix(jax.random.fold_in(key_list[3], 71), 0)
    row_perm = draw_row_perm(jax.random.fold_in(key_list[3], 71), 0)
    block_pattern = draw_block_pattern(jax.random.fold_in(key_list[3], 71), 0)
    return {"matrix": matrix, "row_perm": row_perm, "block_pattern": block_pattern}


def newton_inverse(diagonal_block):
    pivots = jnp.diagonal(diagonal_block)
    inverse = jnp.diag(1.0 / pivots)
    identity = jnp.eye(diagonal_block.shape[0], dtype=jnp.float32)
    for sweep_index in range(NEWTON):
        product = jnp.dot(diagonal_block, inverse, precision=lax.Precision.HIGHEST)
        inverse = jnp.dot(inverse, 2.0 * identity - product, precision=lax.Precision.HIGHEST)
    return inverse


def reference(matrix, row_perm, block_pattern):
    blocks = jnp.transpose(matrix, (1, 0, 2, 4, 3, 5)).reshape(NB, B, NB, B)
    orders = jnp.transpose(row_perm, (1, 0, 2)).reshape(NB, B)
    permuted = jax.vmap(lambda block_row, row_order: block_row[row_order])(blocks, orders)
    current = permuted * block_pattern[:, None, :, None].astype(jnp.bfloat16)
    block_ids = jnp.arange(NB)
    for supernode in range(2):
        inverse = newton_inverse(current[supernode, :, supernode, :].astype(jnp.float32))
        column = current[:, :, supernode, :]
        lower_col = jnp.einsum("irb,bc->irc", column.astype(jnp.float32), inverse, precision=lax.Precision.HIGHEST).astype(jnp.bfloat16)
        below_mask = (block_ids > supernode)[:, None, None]
        lower_used = jnp.where(below_mask, lower_col, jnp.zeros_like(lower_col))
        upper_row = current[supernode]
        right_mask = (block_ids > supernode)[None, :, None]
        upper_used = jnp.where(right_mask, upper_row, jnp.zeros_like(upper_row)).reshape(B, NB * B)

        def update_row(entries):
            block_row, left_block = entries
            product = jnp.dot(left_block, upper_used, preferred_element_type=jnp.float32)
            updated = block_row.reshape(B, NB * B).astype(jnp.float32) - product
            return updated.astype(jnp.bfloat16).reshape(B, NB, B)

        current = lax.map(update_row, (current, lower_used))
        current = current.at[:, :, supernode, :].set(jnp.where(below_mask, lower_col, current[:, :, supernode, :]))
    return jnp.transpose(current.reshape(LR, N_PROW, B, LC, N_PCOL, B), (1, 0, 2, 4, 3, 5))
```

```python
import functools

import jax
import jax.numpy as jnp
from jax import lax
from jax.experimental import pallas as pl
from jax.experimental.pallas import tpu as pltpu
from jax.sharding import PartitionSpec as P

B = 256
LR = 3
LC = 12
UCAP = 6
NEWTON = 3
ROWS_GRID = 32
COLS_GRID = 8
NX = 4
NZ = 8
PIECE = B // NX
MIB = 1 << 20

F32 = jnp.float32
BF16 = jnp.bfloat16

FAR_UP = [(0, 3), (1, 4)]
FAR_DOWN = [(0, 5), (1, 6)]
NEAR_UP = [(0, 1), (3, 4), (5, 6), (1, 2), (4, 5), (6, 7)]
NEAR_DOWN = [(0, 7), (3, 2), (1, 0), (4, 3)]
FROM_0 = "hudhuhud"
FROM_1 = "dhudhuhu"


def one_hot_rows(order):
    source = lax.broadcasted_iota(jnp.int32, (B, B), 0)
    return jnp.where(source == order, 1.0, 0.0).T.astype(BF16)


def split(value, parts):
    out = []
    for _ in range(parts):
        head = value.astype(BF16)
        out.append(head)
        value = value - head.astype(F32)
    return out


def dot(a, b):
    return jnp.dot(a, b, preferred_element_type=F32)


def pack_kernel(pattern_ref, order_ref, blocks_ref, packed_ref, first_ref):
    supernode = jnp.minimum(lax.axis_index("prow"), 1)
    grid_col = lax.axis_index("pcol")
    pick = one_hot_rows(order_ref[0:1, :])
    first = dot(pick, blocks_ref[0, 0])
    present = pattern_ref[supernode, grid_col] != 0
    first_ref[...] = jnp.where(present, first, 0.0).astype(BF16)
    slot = jnp.int32(0)
    for u in range(LC):
        col = grid_col + u * COLS_GRID
        used = (pattern_ref[supernode, col] != 0) & (col > supernode)

        @pl.when(used)
        def _(u=u, slot=slot):
            block = dot(pick, blocks_ref[0, u]).astype(BF16)
            for piece in range(NX):
                packed_ref[piece, slot] = block[piece * PIECE : (piece + 1) * PIECE]

        slot = slot + used.astype(jnp.int32)


def permute_kernel(pattern_ref, order_ref, blocks_ref, out_ref):
    t = pl.program_id(0)
    row = t * ROWS_GRID + lax.axis_index("prow")
    grid_col = lax.axis_index("pcol")
    pick = one_hot_rows(order_ref[pl.ds(t, 1), :])
    for u in range(LC):
        present = pattern_ref[row, grid_col + u * COLS_GRID] != 0

        @pl.when(present)
        def _(u=u):
            out_ref[0, u] = dot(pick, blocks_ref[0, u]).astype(BF16)

        @pl.when(jnp.logical_not(present))
        def _(u=u):
            out_ref[0, u] = jnp.zeros((B, B), BF16)


def inverse_kernel(held_ref, up_ref, down_ref, column_ref, lower_ref, first_ref, high_ref, low_ref):
    grid_row = lax.axis_index("prow")
    grid_col = lax.axis_index("pcol")
    z = grid_row % NZ

    def chosen(table):
        def of(letter, ref):
            hit = functools.reduce(jnp.logical_or, [z == i for i in range(NZ) if table[i] == letter])
            return hit, ref

        (held, h), (up, u) = of("h", held_ref), of("u", up_ref)
        return jnp.where(
            held, h[...].astype(F32), jnp.where(up, u[...].astype(F32), down_ref[...].astype(F32))
        )

    @pl.when(grid_col < 2)
    def _():
        first = chosen(FROM_0)
        first_ref[...] = first.astype(BF16)
        block = jnp.where(grid_col == 0, first, chosen(FROM_1))
        diagonal = lax.broadcasted_iota(jnp.int32, (B, B), 0) == lax.broadcasted_iota(jnp.int32, (B, B), 1)
        pivots = jnp.where(diagonal, block, 0.0)
        by_col = 1.0 / jnp.sum(pivots, axis=0, keepdims=True)
        by_row = 1.0 / jnp.sum(pivots, axis=1, keepdims=True)
        twice = jnp.where(diagonal, 2.0, 0.0)
        inverse = by_row * (twice - block * by_col)
        block16 = block.astype(BF16)
        for _ in range(NEWTON - 1):
            high, middle, low = split(inverse, 3)
            rest = twice - (dot(block16, high) + (dot(block16, middle) + dot(block16, low)))
            rest_high, rest_low = split(rest, 2)
            inverse = dot(high, rest_high) + (dot(high, rest_low) + dot(middle, rest_high))
        high, low = split(inverse, 2)
        high_ref[...] = high
        low_ref[...] = low
        for t in range(LR):
            column = column_ref[t, 0]
            lower = dot(column, high) + dot(column, low)
            lower_ref[t] = jnp.where(t * ROWS_GRID + grid_row > 0, lower, 0.0).astype(BF16)


def second_kernel(lower_ref, first_ref, high_ref, low_ref, column_ref, out_ref):
    grid_row = lax.axis_index("prow")

    @pl.when(lax.axis_index("pcol") == 1)
    def _():
        for t in range(LR):
            column = (column_ref[t, 0].astype(F32) - dot(lower_ref[t], first_ref[...])).astype(BF16)
            lower = dot(column, high_ref[...]) + dot(column, low_ref[...])
            out_ref[t] = jnp.where(t * ROWS_GRID + grid_row > 1, lower, 0.0).astype(BF16)


def schur_kernel(
    pattern_ref, own_ref, one_ref, two_ref, three_ref, low0e_ref, low0o_ref, low1e_ref, low1o_ref, in_ref, out_ref,
    upper, lower, work, upper_sem, lower_sem, in_sem, out_sem,
):
    del in_ref
    grid_row = lax.axis_index("prow")
    grid_col = lax.axis_index("pcol")
    x = grid_row // NZ

    def plan(u):
        col = grid_col + u * COLS_GRID
        use0 = (pattern_ref[0, col] != 0) & (col > 0)
        use1 = (pattern_ref[1, col] != 0) & (col > 1)
        return use0, use1, use0 | use1 | (col < 2)

    def fetch(u):
        return pltpu.make_async_copy(out_ref.at[:, u], work.at[u], in_sem.at[u])

    def store(u):
        return pltpu.make_async_copy(work.at[u], out_ref.at[:, u], out_sem.at[u])

    lowers = [
        [pltpu.make_async_copy(src, lower.at[k], lower_sem.at[k]) for k, src in enumerate(pair)]
        for pair in ((low0e_ref, low1e_ref), (low0o_ref, low1o_ref))
    ]
    for parity in range(2):

        @pl.when(grid_col % 2 == parity)
        def _(parity=parity):
            for copy in lowers[parity]:
                copy.start()

    uppers = []
    for shift, ref in enumerate((own_ref, one_ref, two_ref, three_ref)):
        rows = pl.ds(pl.multiple_of((x + NX - shift) % NX * PIECE, PIECE), PIECE)
        uppers.append(pltpu.make_async_copy(ref, upper.at[:, :, rows, :], upper_sem.at[shift]))
    for copy in uppers:
        copy.start()

    def start_fetch(u, carry):
        @pl.when(plan(u)[2])
        def _():
            fetch(u).start()

        return carry

    lax.fori_loop(0, LC, start_fetch, 0)
    for parity in range(2):

        @pl.when(grid_col % 2 == parity)
        def _(parity=parity):
            for copy in lowers[parity]:
                copy.wait()

    for copy in uppers:
        copy.wait()

    def step(u, slots):
        use0, use1, touched = plan(u)
        slot0, slot1 = slots

        @pl.when(touched)
        def _():
            fetch(u).wait()

            def update(k, slot):
                for t in range(LR):
                    product = dot(lower[k, t], upper[k, slot])
                    work[u, t] = (work[u, t].astype(F32) - product).astype(BF16)

            @pl.when(use0)
            def _():
                update(0, slot0)

            @pl.when(use1)
            def _():
                update(1, slot1)

            for k in range(2):

                @pl.when((u == 0) & (grid_col == k))
                def _(k=k):
                    for t in range(LR):

                        @pl.when(t * ROWS_GRID + grid_row > k)
                        def _(t=t):
                            work[0, t] = lower[k, t]

            store(u).start()

        return slot0 + use0.astype(jnp.int32), slot1 + use1.astype(jnp.int32)

    lax.fori_loop(0, LC, step, (jnp.int32(0), jnp.int32(0)))

    def finish(u, carry):
        @pl.when(plan(u)[2])
        def _():
            store(u).wait()

        return carry

    lax.fori_loop(0, LC, finish, 0)


def pick_by(index, options):
    value = None
    for i, option in enumerate(options):
        if option is not None:
            value = option if value is None else jnp.where(index == i, option, value)
    return value


def along_z(pairs, cols):
    rows = [(x * NZ + a, x * NZ + b) for x in range(NX) for a, b in pairs]
    if cols is None:
        return rows
    return [(a * COLS_GRID + c, b * COLS_GRID + c) for a, b in rows for c in cols]


def from_x0(shift, cols):
    rows = [(z, shift * NZ + z) for z in range(2)]
    if cols is None:
        return rows
    return [(a * COLS_GRID + c, b * COLS_GRID + c) for a, b in rows for c in cols]


def spread(sent, x, z, cols):
    axes = "prow" if cols is None else ("prow", "pcol")
    got = [sent[0]] + [lax.ppermute(sent[d], axes, from_x0(d, cols)) for d in range(1, NX)]
    mine = pick_by(x, got)
    far_up = lax.ppermute(mine, axes, along_z(FAR_UP, cols))
    far_down = lax.ppermute(mine, axes, along_z(FAR_DOWN, cols))
    held = pick_by(z, [mine, None, None, far_up, far_up, far_down, far_down, None])
    up = lax.ppermute(held, axes, along_z(NEAR_UP, cols))
    down = lax.ppermute(held, axes, along_z(NEAR_DOWN, cols))
    return held, up, down


def vmem():
    return pl.BlockSpec(memory_space=pltpu.VMEM)


def smem():
    return pl.BlockSpec(memory_space=pltpu.SMEM)


def anywhere():
    return pl.BlockSpec(memory_space=pl.ANY)


def like(*shape):
    return jax.ShapeDtypeStruct(shape, BF16)


def params(limit):
    return pltpu.CompilerParams(vmem_limit_bytes=limit * MIB)


def cost(flops, moved):
    return pl.CostEstimate(flops=flops, bytes_accessed=moved, transcendentals=0)


def local(matrix, row_perm, block_pattern):
    grid_row = lax.axis_index("prow")
    grid_col = lax.axis_index("pcol")
    x, z = grid_row // NZ, grid_row % NZ
    blocks = jnp.transpose(matrix[0, :, :, 0], (0, 2, 1, 3))
    orders = row_perm[0]
    block = B * B * 2

    packed, first = pl.pallas_call(
        pack_kernel,
        out_shape=(like(NX, UCAP, PIECE, B), like(B, B)),
        grid=(1,),
        in_specs=[smem(), vmem(), pl.BlockSpec((1, LC, B, B), lambda i: (0, 0, 0, 0))],
        out_specs=(vmem(), vmem()),
        compiler_params=params(16),
        cost_estimate=cost(2 * 7 * B**3, 19 * block),
        name="pack",
    )(block_pattern, orders, blocks)

    column_shape = pl.BlockSpec((LR, 1, B, B), lambda i: (0, 0, 0, 0))
    early = spread([first] * NX, x, z, (0, 1))
    upper = spread([packed[d] for d in range(NX)], x, z, None)

    current = pl.pallas_call(
        permute_kernel,
        out_shape=like(LR, LC, B, B),
        grid=(LR,),
        in_specs=[smem(), vmem(), pl.BlockSpec((1, LC, B, B), lambda t: (t, 0, 0, 0))],
        out_specs=pl.BlockSpec((1, LC, B, B), lambda t: (t, 0, 0, 0)),
        compiler_params=params(24),
        cost_estimate=cost(2 * LR * LC * B**3, 2 * LR * LC * block),
        name="permute",
    )(block_pattern, orders, blocks)

    lower0, first0, high, low = pl.pallas_call(
        inverse_kernel,
        out_shape=(like(LR, B, B), like(B, B), like(B, B), like(B, B)),
        grid=(1,),
        in_specs=[vmem(), vmem(), vmem(), column_shape],
        out_specs=(vmem(), vmem(), vmem(), vmem()),
        compiler_params=params(16),
        cost_estimate=cost(2 * 18 * B**3, 12 * block),
        name="inverse",
    )(*early, current)

    neighbour0 = lax.ppermute(lower0, "pcol", [(0, 1)])
    lower1 = pl.pallas_call(
        second_kernel,
        out_shape=like(LR, B, B),
        grid=(1,),
        in_specs=[vmem(), vmem(), vmem(), vmem(), column_shape],
        out_specs=vmem(),
        compiler_params=params(16),
        cost_estimate=cost(2 * 9 * B**3, 12 * block),
        name="second",
    )(neighbour0, first0, high, low, current)

    def along_y(lower, core):
        got = [lower] + [lax.ppermute(lower, "pcol", [(core, 2 * d + core)]) for d in range(1, COLS_GRID // 2)]
        return pick_by(grid_col // 2, got)

    lower0_even = along_y(lower0, 0)
    lower0_odd = lax.ppermute(lower0_even, "pcol", [(c, c + 1) for c in range(0, COLS_GRID, 2)])
    lower1_odd = along_y(lower1, 1)
    lower1_even = lax.ppermute(lower1_odd, "pcol", [(c + 1, c) for c in range(0, COLS_GRID, 2)])

    held, up, down = upper
    letters = {"h": held, "u": up, "d": down}
    own = jnp.stack([pick_by(z, [letters[c] for c in table]) for table in (FROM_0, FROM_1)])
    by_x = [
        lax.ppermute(own, "prow", [(r, (r + d * NZ) % ROWS_GRID) for r in range(ROWS_GRID)]) for d in range(1, NX)
    ]

    current = pl.pallas_call(
        schur_kernel,
        out_shape=like(LR, LC, B, B),
        in_specs=[smem()] + [anywhere()] * 9,
        out_specs=anywhere(),
        scratch_shapes=[
            pltpu.VMEM((2, UCAP, B, B), BF16),
            pltpu.VMEM((2, LR, B, B), BF16),
            pltpu.VMEM((LC, LR, B, B), BF16),
            pltpu.SemaphoreType.DMA((NX,)),
            pltpu.SemaphoreType.DMA((2,)),
            pltpu.SemaphoreType.DMA((LC,)),
            pltpu.SemaphoreType.DMA((LC,)),
        ],
        input_output_aliases={9: 0},
        compiler_params=params(24),
        cost_estimate=cost(2 * LR * 12 * B**3, 90 * block),
        name="schur",
    )(block_pattern, own, *by_x, lower0_even, lower0_odd, lower1_even, lower1_odd, current)
    return jnp.transpose(current, (0, 2, 1, 3)).reshape(matrix.shape)


def solution(mesh):
    placed = (P("prow", None, None, "pcol", None, None), P("prow", None, None), P())
    return jax.shard_map(
        local,
        mesh=mesh,
        in_specs=placed,
        out_specs=P("prow", None, None, "pcol", None, None),
        check_vma=False,
    )
```

```python
import functools

import jax
import jax.numpy as jnp
from jax import lax
from jax.experimental import pallas as pl
from jax.experimental.pallas import tpu as pltpu
from jax.sharding import PartitionSpec as P

B = 256
LR = 3
LC = 12
NB = 96
UCAP = 6
NEWTON = 3
ROWS_GRID = 32
COLS_GRID = 8
NX = 4
NZ = 8
PIECE = B // NX
SELECT_BYTES = 8 << 20
MIB = 1 << 20

F32 = jnp.float32
BF16 = jnp.bfloat16

FAR_UP = [(0, 3), (1, 4)]
FAR_DOWN = [(0, 5), (1, 6)]
NEAR_UP = [(0, 1), (3, 4), (5, 6), (1, 2), (4, 5), (6, 7)]
NEAR_DOWN = [(0, 7), (3, 2), (1, 0), (4, 3)]
FROM_0 = "hudhuhud"
FROM_1 = "dhudhuhu"
SKIPS = (2, -2, 4)
SKIP_OF = (0, 0, 1, 1, 3, 3, 2, 2)
HELD_ROW = (0, 1) * (NZ // 2)


def skip_z(skip):
    return [(z, (z + skip) % NZ) for z in range(2)]


def ring_z(step):
    return [(z, (z + step) % NZ) for z in range(NZ)]


def one_hot_rows(order):
    source = lax.broadcasted_iota(jnp.int32, (B, B), 0)
    return jnp.where(source == order, 1.0, 0.0).T.astype(BF16)


def split(value, parts):
    out = []
    for _ in range(parts):
        head = value.astype(BF16)
        out.append(head)
        value = value - head.astype(F32)
    return out


def dot(a, b):
    return jnp.dot(a, b, preferred_element_type=F32)


def pack_kernel(pattern_hbm, order_hbm, blocks_hbm, packed_ref, first_ref, pattern, order, blocks, sem, block_sem):
    small = [
        pltpu.make_async_copy(order_hbm.at[0], order, sem.at[0]),
        pltpu.make_async_copy(pattern_hbm.at[0:8], pattern, sem.at[1]),
    ]
    fetches = [pltpu.make_async_copy(blocks_hbm.at[0, u], blocks.at[u], block_sem.at[u]) for u in range(LC)]
    for copy in small + fetches:
        copy.start()
    for copy in small:
        copy.wait()
    supernode = jnp.minimum(lax.axis_index("prow"), 1)
    grid_col = lax.axis_index("pcol")
    pick = one_hot_rows(order[...])
    slot = jnp.int32(0)
    chosen = [jnp.int32(0)] * UCAP
    for u in range(LC):
        col = grid_col + u * COLS_GRID
        used = (pattern[supernode, col] != 0) & (col > supernode)
        chosen = [jnp.where(used & (slot == s), u, c) for s, c in enumerate(chosen)]
        slot = slot + used.astype(jnp.int32)
    for copy in fetches:
        copy.wait()
    present = pattern[supernode, grid_col] != 0
    first_ref[...] = jnp.where(present, dot(pick, blocks[0]), 0.0).astype(BF16)
    for s, u in enumerate(chosen):
        block = dot(pick, blocks[u]).astype(BF16)
        for piece in range(NX):
            packed_ref[piece, s] = block[piece * PIECE : (piece + 1) * PIECE]


def permute_kernel(t, pattern_hbm, order_hbm, blocks_hbm, after, placed_ref, pattern, order, blocks, sem, block_sem):
    del after
    row = t * ROWS_GRID + lax.axis_index("prow")
    grid_col = lax.axis_index("pcol")
    small = [
        pltpu.make_async_copy(order_hbm.at[t], order, sem.at[0]),
        pltpu.make_async_copy(pattern_hbm.at[pl.ds(pl.multiple_of(row // 8 * 8, 8), 8)], pattern, sem.at[1]),
    ]
    fetches = [pltpu.make_async_copy(blocks_hbm.at[t, u], blocks.at[u], block_sem.at[u]) for u in range(LC)]
    for copy in small + fetches:
        copy.start()
    for copy in small:
        copy.wait()
    pick = one_hot_rows(order[...])
    for copy in fetches:
        copy.wait()
    for u in range(LC):
        present = pattern[row % 8, grid_col + u * COLS_GRID] != 0
        placed_ref[u] = jnp.where(present, dot(pick, blocks[u]), 0.0).astype(BF16)


def select_kernel(choices, *refs):
    *options, out_ref = refs
    part, table = choices
    grid_row = lax.axis_index("prow")
    place = {"x": grid_row // NZ, "z": grid_row % NZ, "y": lax.axis_index("pcol") // 2}[part]
    for i in range(max(table) + 1):
        hit = functools.reduce(jnp.logical_or, [place == p for p, choice in enumerate(table) if choice == i])

        @pl.when(hit)
        def _(i=i):
            out_ref[...] = options[i][...]


def inverse_kernel(
    held_ref, up_ref, down_ref, pattern_hbm, order_hbm, blocks_hbm, after,
    lower_ref, first_ref, high_ref, low_ref, column_ref,
    pattern, orders, blocks, sem, pattern_sem,
):
    del after
    grid_row = lax.axis_index("prow")
    grid_col = lax.axis_index("pcol")
    z = grid_row % NZ

    def chosen(table):
        def of(letter, ref):
            hit = functools.reduce(jnp.logical_or, [z == i for i in range(NZ) if table[i] == letter])
            return hit, ref

        (held, h), (up, u) = of("h", held_ref), of("u", up_ref)
        return jnp.where(
            held, h[...].astype(F32), jnp.where(up, u[...].astype(F32), down_ref[...].astype(F32))
        )

    @pl.when(grid_col < 2)
    def _():
        fetches = [
            pltpu.make_async_copy(order_hbm, orders, sem.at[0]),
            pltpu.make_async_copy(blocks_hbm.at[:, 0], blocks, sem.at[1]),
        ]
        for t in range(LR):
            group = pl.ds(pl.multiple_of((t * ROWS_GRID + grid_row) // 8 * 8, 8), 8)
            fetches.append(pltpu.make_async_copy(pattern_hbm.at[group], pattern.at[t], pattern_sem.at[t]))
        for copy in fetches:
            copy.start()
        first = chosen(FROM_0)
        first_ref[...] = first.astype(BF16)
        block = jnp.where(grid_col == 0, first, chosen(FROM_1))
        diagonal = lax.broadcasted_iota(jnp.int32, (B, B), 0) == lax.broadcasted_iota(jnp.int32, (B, B), 1)
        pivots = jnp.where(diagonal, block, 0.0)
        by_col = 1.0 / jnp.sum(pivots, axis=0, keepdims=True)
        by_row = 1.0 / jnp.sum(pivots, axis=1, keepdims=True)
        twice = jnp.where(diagonal, 2.0, 0.0)
        inverse = by_row * (twice - block * by_col)
        block16 = block.astype(BF16)
        for _ in range(NEWTON - 1):
            high, middle, low = split(inverse, 3)
            rest = twice - (dot(block16, high) + (dot(block16, middle) + dot(block16, low)))
            rest_high, rest_low = split(rest, 2)
            inverse = dot(high, rest_high) + (dot(high, rest_low) + dot(middle, rest_high))
        high, low = split(inverse, 2)
        high_ref[...] = high
        low_ref[...] = low
        for copy in fetches:
            copy.wait()
        for t in range(LR):
            present = pattern[t, grid_row % 8, grid_col] != 0
            column = jnp.where(present, dot(one_hot_rows(orders[t]), blocks[t]), 0.0).astype(BF16)
            column_ref[t] = column
            lower = dot(column, high) + dot(column, low)
            lower_ref[t] = jnp.where(t * ROWS_GRID + grid_row > 0, lower, 0.0).astype(BF16)


def second_kernel(own_ref, lower_ref, first_ref, high_ref, low_ref, column_ref, out_ref):
    grid_row = lax.axis_index("prow")

    @pl.when(lax.axis_index("pcol") == 0)
    def _():
        out_ref[...] = own_ref[...]

    @pl.when(lax.axis_index("pcol") == 1)
    def _():
        for t in range(LR):
            rest = (column_ref[t].astype(F32) - dot(lower_ref[t], first_ref[...])).astype(BF16)
            lower = dot(rest, high_ref[...]) + dot(rest, low_ref[...])
            out_ref[t] = jnp.where(t * ROWS_GRID + grid_row > 1, lower, 0.0).astype(BF16)


def schur_kernel(
    pattern_hbm, held0, held1, held2, held3, other01, other23, mine_ref, neighbour_ref, row0, row1, row2,
    out_hbm, pattern, upper, lower, work, sem, upper_sem, lower_sem, out_sem,
):
    rows = (row0, row1, row2)
    grid_row = lax.axis_index("prow")
    grid_col = lax.axis_index("pcol")
    x, z = grid_row // NZ, grid_row % NZ
    held_row = functools.reduce(jnp.logical_or, [z == i for i in range(NZ) if HELD_ROW[i]]).astype(jnp.int32)

    def plan(u):
        col = grid_col + u * COLS_GRID
        use0 = (pattern[0, col] != 0) & (col > 0)
        use1 = (pattern[1, col] != 0) & (col > 1)
        return use0, use1, use0 | use1 | (col < 2)

    def store(u):
        return pltpu.make_async_copy(work.at[u], out_hbm.at[:, u], out_sem.at[u])

    def passed(u):
        return [pltpu.make_async_copy(rows[t].at[u], out_hbm.at[t, u], out_sem.at[u]) for t in range(LR)]

    rows_of = pltpu.make_async_copy(pattern_hbm.at[0:8], pattern, sem)
    rows_of.start()
    operands = [
        pltpu.make_async_copy(mine_ref, lower.at[grid_col % 2], lower_sem.at[0]),
        pltpu.make_async_copy(neighbour_ref, lower.at[1 - grid_col % 2], lower_sem.at[1]),
    ]
    for k, refs in ((held_row, (held0, held1, held2, held3)), (1 - held_row, [pair.at[i] for pair in (other01, other23) for i in range(2)])):
        for shift, ref in enumerate(refs):
            part = pl.ds(pl.multiple_of((x + NX - shift) % NX * PIECE, PIECE), PIECE)
            operands.append(pltpu.make_async_copy(ref, upper.at[k, :, part, :], upper_sem.at[len(operands)]))
    for copy in operands:
        copy.start()
    rows_of.wait()

    def start_passed(u, carry):
        @pl.when(jnp.logical_not(plan(u)[2]))
        def _():
            for copy in passed(u):
                copy.start()

        return carry

    lax.fori_loop(0, LC, start_passed, 0)
    for copy in operands:
        copy.wait()

    def step(u, slots):
        use0, use1, touched = plan(u)
        slot0, slot1 = slots

        @pl.when(touched)
        def _():
            for t in range(LR):
                work[u, t] = rows[t][u]

            def update(k, slot):
                product = dot(lower[k].reshape(LR * B, B), upper[k, slot]).reshape(LR, B, B)
                work[u] = (work[u].astype(F32) - product).astype(BF16)

            @pl.when(use0)
            def _():
                update(0, slot0)

            @pl.when(use1)
            def _():
                update(1, slot1)

            for k in range(2):

                @pl.when((u == 0) & (grid_col == k))
                def _(k=k):
                    for t in range(LR):

                        @pl.when(t * ROWS_GRID + grid_row > k)
                        def _(t=t):
                            work[0, t] = lower[k, t]

            store(u).start()

        return slot0 + use0.astype(jnp.int32), slot1 + use1.astype(jnp.int32)

    lax.fori_loop(0, LC, step, (jnp.int32(0), jnp.int32(0)))

    def finish(u, carry):
        store(u).wait()
        return carry

    lax.fori_loop(0, LC, finish, 0)


def pick_by(index, options):
    value = None
    for i, option in enumerate(options):
        if option is not None:
            value = option if value is None else jnp.where(index == i, option, value)
    return value


def along_z(pairs, cols):
    rows = [(x * NZ + a, x * NZ + b) for x in range(NX) for a, b in pairs]
    if cols is None:
        return rows
    return [(a * COLS_GRID + c, b * COLS_GRID + c) for a, b in rows for c in cols]


def from_x0(shift, cols):
    rows = [(z, shift * NZ + z) for z in range(2)]
    if cols is None:
        return rows
    return [(a * COLS_GRID + c, b * COLS_GRID + c) for a, b in rows for c in cols]


def scattered(sent, cols):
    axes = "prow" if cols is None else ("prow", "pcol")
    return [sent[0]] + [lax.ppermute(sent[d], axes, from_x0(d, cols)) for d in range(1, NX)]


def select(part, table, *options, after=()):
    return pl.pallas_call(
        functools.partial(select_kernel, (part, tuple(table))),
        out_shape=jax.ShapeDtypeStruct(options[0].shape, options[0].dtype),
        in_specs=[vmem()] * len(options) + [anywhere()] * len(after),
        out_specs=vmem(),
        compiler_params=params(8),
        cost_estimate=cost(0, SELECT_BYTES),
        name="select",
    )(*options, *after)


def spread_whole(first, x, cols, after):
    axes = ("prow", "pcol")
    mine = pick_by(x, scattered([first] * NX, cols))
    far_up = lax.ppermute(mine, axes, along_z(FAR_UP, cols))
    far_down = lax.ppermute(mine, axes, along_z(FAR_DOWN, cols))
    held = select("z", (0, 0, 0, 1, 1, 2, 2, 0), mine, far_up, far_down, after=after)
    up = lax.ppermute(held, axes, along_z(NEAR_UP, cols))
    down = lax.ppermute(held, axes, along_z(NEAR_DOWN, cols))
    return held, up, down


def gather_x(own):
    shifted = [[(r, (r + d * NZ) % ROWS_GRID) for r in range(ROWS_GRID)] for d in range(1, NX)]
    return [own] + [lax.ppermute(own, "prow", pairs) for pairs in shifted]


def vmem():
    return pl.BlockSpec(memory_space=pltpu.VMEM)


def hbm():
    return pl.BlockSpec(memory_space=pltpu.HBM)


def in_hbm(value):
    return pltpu.with_memory_space_constraint(value, pltpu.HBM)


def anywhere():
    return pl.BlockSpec(memory_space=pl.ANY)


def like(*shape):
    return jax.ShapeDtypeStruct(shape, BF16)


def params(limit):
    return pltpu.CompilerParams(vmem_limit_bytes=limit * MIB)


def cost(flops, moved):
    return pl.CostEstimate(flops=flops, bytes_accessed=moved, transcendentals=0)


def local(matrix, row_perm, block_pattern):
    grid_row = lax.axis_index("prow")
    grid_col = lax.axis_index("pcol")
    x, z = grid_row // NZ, grid_row % NZ
    blocks = in_hbm(jnp.transpose(matrix[0, :, :, 0], (0, 2, 1, 3)))
    orders = in_hbm(row_perm.reshape(LR, 1, B))
    block_pattern = in_hbm(block_pattern)
    block = B * B * 2
    small_scratch = [pltpu.SMEM((8, NB), jnp.int32), pltpu.VMEM((1, B), jnp.int32)]
    dma = pltpu.SemaphoreType.DMA

    def permute(t, after):
        return pl.pallas_call(
            functools.partial(permute_kernel, t),
            out_shape=pltpu.VMEM((LC, B, B), BF16),
            in_specs=[hbm()] * 3 + [anywhere()],
            out_specs=vmem(),
            scratch_shapes=small_scratch + [pltpu.VMEM((LC, B, B), BF16), dma((2,)), dma((LC,))],
            compiler_params=params(16),
            cost_estimate=cost(2 * LC * B**3, 2 * LC * block),
            name="permute",
        )(block_pattern, orders, blocks, after)

    packed, first = pl.pallas_call(
        pack_kernel,
        out_shape=(like(NX, UCAP, PIECE, B), like(B, B)),
        in_specs=[hbm(), hbm(), hbm()],
        out_specs=(vmem(), vmem()),
        scratch_shapes=small_scratch + [pltpu.VMEM((LC, B, B), BF16), dma((2,)), dma((LC,))],
        compiler_params=params(16),
        cost_estimate=cost(2 * 7 * B**3, 19 * block),
        name="pack",
    )(block_pattern, orders, blocks)

    mine = select("x", range(NX), *scattered([packed[d] for d in range(NX)], None))
    held, up, down = spread_whole(first, x, (0, 1), (mine,))
    skipped = [lax.ppermute(mine, "prow", along_z(skip_z(skip), None)) for skip in SKIPS]
    placed = [permute(0, held)]
    held_row = select("z", SKIP_OF, mine, *skipped, after=placed)
    held_rows = gather_x(held_row)
    other_rows = [
        lax.ppermute(jnp.stack(held_rows[i : i + 2]), "prow", along_z(ring_z(step), None)) for i, step in ((0, 1), (2, -1))
    ]

    lower0, first0, high, low, column = pl.pallas_call(
        inverse_kernel,
        out_shape=(like(LR, B, B), like(B, B), like(B, B), like(B, B), like(LR, B, B)),
        in_specs=[vmem(), vmem(), vmem(), hbm(), hbm(), hbm(), anywhere()],
        out_specs=(vmem(),) * 5,
        scratch_shapes=[
            pltpu.SMEM((LR, 8, NB), jnp.int32),
            pltpu.VMEM((LR, 1, B), jnp.int32),
            pltpu.VMEM((LR, B, B), BF16),
            dma((2,)),
            dma((LR,)),
        ],
        compiler_params=params(16),
        cost_estimate=cost(2 * 18 * B**3, 12 * block),
        name="inverse",
    )(held, up, down, block_pattern, orders, blocks, held_row)

    neighbour0 = lax.ppermute(lower0, "pcol", [(0, 1)])
    lower = pl.pallas_call(
        second_kernel,
        out_shape=like(LR, B, B),
        in_specs=[vmem()] * 6,
        out_specs=vmem(),
        compiler_params=params(16),
        cost_estimate=cost(2 * 9 * B**3, 12 * block),
        name="second",
    )(lower0, neighbour0, first0, high, low, column)

    placed += [permute(t, lower) for t in range(1, LR)]
    got = [lax.ppermute(lower, "pcol", [(0, 2 * d), (1, 2 * d + 1)]) for d in range(1, COLS_GRID // 2)]
    lower_mine = select("y", range(4), lower, *got, after=placed[1:])
    lower_neighbour = lax.ppermute(lower_mine, "pcol", [(c, c ^ 1) for c in range(COLS_GRID)])

    current = pl.pallas_call(
        schur_kernel,
        out_shape=like(LR, LC, B, B),
        in_specs=[hbm()] + [anywhere()] * (NX + 4) + [vmem()] * LR,
        out_specs=hbm(),
        scratch_shapes=[
            pltpu.SMEM((8, NB), jnp.int32),
            pltpu.VMEM((2, UCAP, B, B), BF16),
            pltpu.VMEM((2, LR, B, B), BF16),
            pltpu.VMEM((LC, LR, B, B), BF16),
            dma,
            dma((2 * NX + 2,)),
            dma((2,)),
            dma((LC,)),
        ],
        compiler_params=params(24),
        cost_estimate=cost(2 * LR * 12 * B**3, 90 * block),
        name="schur",
    )(block_pattern, *held_rows, *other_rows, lower_mine, lower_neighbour, *placed)
    return jnp.transpose(current, (0, 2, 1, 3)).reshape(matrix.shape)


def solution(mesh):
    placed = (P("prow", None, None, "pcol", None, None), P("prow", None, None), P())
    return jax.shard_map(
        local,
        mesh=mesh,
        in_specs=placed,
        out_specs=P("prow", None, None, "pcol", None, None),
        check_vma=False,
    )
```

```python
import functools

import jax
import jax.numpy as jnp
from jax import lax
from jax.experimental import pallas as pl
from jax.experimental.pallas import tpu as pltpu
from jax.sharding import PartitionSpec as P

B = 256
LR = 3
LC = 12
NB = 96
UCAP = 6
NEWTON = 3
ROWS_GRID = 32
COLS_GRID = 8
NX = 4
NZ = 8
PIECE = B // NX
SELECT_BYTES = 8 << 20
MIB = 1 << 20

F32 = jnp.float32
BF16 = jnp.bfloat16

FAR_UP = ([(0, 3)], [(1, 4)])
FAR_DOWN = ([(0, 5)], [(1, 6)])
NEAR_UP = ([(0, 1), (3, 4), (5, 6)], [(1, 2), (4, 5), (6, 7)])
NEAR_DOWN = ([(0, 7), (3, 2)], [(1, 0), (4, 3)])
FROM_0 = "hudhuhud"
FROM_1 = "dhudhuhu"
SKIPS = (2, -2, 4)
SKIP_OF = (0, 0, 1, 1, 3, 3, 2, 2)
HELD_ROW = (0, 1) * (NZ // 2)


def skip_z(skip):
    return [(z, (z + skip) % NZ) for z in range(2)]


def ring_z(step):
    return [(z, (z + step) % NZ) for z in range(NZ)]


def one_hot_rows(order):
    source = lax.broadcasted_iota(jnp.int32, (B, B), 0)
    return jnp.where(source == order, 1.0, 0.0).T.astype(BF16)


def split(value, parts):
    out = []
    for _ in range(parts):
        head = value.astype(BF16)
        out.append(head)
        value = value - head.astype(F32)
    return out


def dot(a, b):
    return jnp.dot(a, b, preferred_element_type=F32)


def pack_kernel(pattern_hbm, order_hbm, blocks_hbm, packed_ref, first_ref, pattern, order, blocks, sem, block_sem):
    small = [
        pltpu.make_async_copy(order_hbm.at[0], order, sem.at[0]),
        pltpu.make_async_copy(pattern_hbm.at[0:8], pattern, sem.at[1]),
    ]
    fetches = [pltpu.make_async_copy(blocks_hbm.at[0, u], blocks.at[u], block_sem.at[u]) for u in range(LC)]
    for copy in small + fetches:
        copy.start()
    for copy in small:
        copy.wait()
    supernode = jnp.minimum(lax.axis_index("prow"), 1)
    grid_col = lax.axis_index("pcol")
    pick = one_hot_rows(order[...])
    slot = jnp.int32(0)
    chosen = [jnp.int32(0)] * UCAP
    for u in range(LC):
        col = grid_col + u * COLS_GRID
        used = (pattern[supernode, col] != 0) & (col > supernode)
        chosen = [jnp.where(used & (slot == s), u, c) for s, c in enumerate(chosen)]
        slot = slot + used.astype(jnp.int32)
    for copy in fetches:
        copy.wait()
    present = pattern[supernode, grid_col] != 0
    first_ref[...] = jnp.where(present, dot(pick, blocks[0]), 0.0).astype(BF16)
    for s, u in enumerate(chosen):
        block = dot(pick, blocks[u]).astype(BF16)
        for piece in range(NX):
            packed_ref[piece, s] = block[piece * PIECE : (piece + 1) * PIECE]


def permute_kernel(t, pattern_hbm, order_hbm, blocks_hbm, after, placed_ref, pattern, order, blocks, sem, block_sem):
    del after
    row = t * ROWS_GRID + lax.axis_index("prow")
    grid_col = lax.axis_index("pcol")
    small = [
        pltpu.make_async_copy(order_hbm.at[t], order, sem.at[0]),
        pltpu.make_async_copy(pattern_hbm.at[pl.ds(pl.multiple_of(row // 8 * 8, 8), 8)], pattern, sem.at[1]),
    ]
    fetches = [pltpu.make_async_copy(blocks_hbm.at[t, u], blocks.at[u], block_sem.at[u]) for u in range(LC)]
    for copy in small + fetches:
        copy.start()
    for copy in small:
        copy.wait()
    pick = one_hot_rows(order[...])
    for copy in fetches:
        copy.wait()
    for u in range(LC):
        present = pattern[row % 8, grid_col + u * COLS_GRID] != 0
        placed_ref[u] = jnp.where(present, dot(pick, blocks[u]), 0.0).astype(BF16)


def select_kernel(choices, *refs):
    *options, out_ref = refs
    part, table = choices
    grid_row = lax.axis_index("prow")
    place = {"x": grid_row // NZ, "z": grid_row % NZ, "y": lax.axis_index("pcol") // 2}[part]
    for i in range(max(table) + 1):
        hit = functools.reduce(jnp.logical_or, [place == p for p, choice in enumerate(table) if choice == i])

        @pl.when(hit)
        def _(i=i):
            out_ref[...] = options[i][...]


def inverse_kernel(
    held_ref, up_ref, down_ref, pattern_hbm, order_hbm, blocks_hbm, after,
    lower_ref, first_ref, high_ref, low_ref, column_ref,
    pattern, orders, blocks, sem, pattern_sem,
):
    del after
    grid_row = lax.axis_index("prow")
    grid_col = lax.axis_index("pcol")
    z = grid_row % NZ

    def chosen(table):
        def of(letter, ref):
            hit = functools.reduce(jnp.logical_or, [z == i for i in range(NZ) if table[i] == letter])
            return hit, ref

        (held, h), (up, u) = of("h", held_ref), of("u", up_ref)
        return jnp.where(
            held, h[...].astype(F32), jnp.where(up, u[...].astype(F32), down_ref[...].astype(F32))
        )

    @pl.when(grid_col < 2)
    def _():
        fetches = [
            pltpu.make_async_copy(order_hbm, orders, sem.at[0]),
            pltpu.make_async_copy(blocks_hbm.at[:, 0], blocks, sem.at[1]),
        ]
        for t in range(LR):
            group = pl.ds(pl.multiple_of((t * ROWS_GRID + grid_row) // 8 * 8, 8), 8)
            fetches.append(pltpu.make_async_copy(pattern_hbm.at[group], pattern.at[t], pattern_sem.at[t]))
        for copy in fetches:
            copy.start()
        first = chosen(FROM_0)
        first_ref[...] = first.astype(BF16)
        block = jnp.where(grid_col == 0, first, chosen(FROM_1))
        diagonal = lax.broadcasted_iota(jnp.int32, (B, B), 0) == lax.broadcasted_iota(jnp.int32, (B, B), 1)
        pivots = jnp.where(diagonal, block, 0.0)
        by_col = 1.0 / jnp.sum(pivots, axis=0, keepdims=True)
        by_row = 1.0 / jnp.sum(pivots, axis=1, keepdims=True)
        twice = jnp.where(diagonal, 2.0, 0.0)
        inverse = by_row * (twice - block * by_col)
        block16 = block.astype(BF16)
        for _ in range(NEWTON - 1):
            high, middle, low = split(inverse, 3)
            rest = twice - (dot(block16, high) + (dot(block16, middle) + dot(block16, low)))
            rest_high, rest_low = split(rest, 2)
            inverse = dot(high, rest_high) + (dot(high, rest_low) + dot(middle, rest_high))
        high, low = split(inverse, 2)
        high_ref[...] = high
        low_ref[...] = low
        for copy in fetches:
            copy.wait()
        for t in range(LR):
            present = pattern[t, grid_row % 8, grid_col] != 0
            column = jnp.where(present, dot(one_hot_rows(orders[t]), blocks[t]), 0.0).astype(BF16)
            column_ref[t] = column
            lower = dot(column, high) + dot(column, low)
            lower_ref[t] = jnp.where(t * ROWS_GRID + grid_row > 0, lower, 0.0).astype(BF16)


def second_kernel(own_ref, lower_ref, first_ref, high_ref, low_ref, column_ref, out_ref):
    grid_row = lax.axis_index("prow")

    @pl.when(lax.axis_index("pcol") == 0)
    def _():
        out_ref[...] = own_ref[...]

    @pl.when(lax.axis_index("pcol") == 1)
    def _():
        for t in range(LR):
            rest = (column_ref[t].astype(F32) - dot(lower_ref[t], first_ref[...])).astype(BF16)
            lower = dot(rest, high_ref[...]) + dot(rest, low_ref[...])
            out_ref[t] = jnp.where(t * ROWS_GRID + grid_row > 1, lower, 0.0).astype(BF16)


def schur_kernel(
    pattern_hbm, held0, held1, held2, held3, other01, other23, mine_ref, neighbour_ref, row0, row1, row2,
    out_hbm, pattern, upper, lower, work, sem, upper_sem, lower_sem, out_sem,
):
    rows = (row0, row1, row2)
    grid_row = lax.axis_index("prow")
    grid_col = lax.axis_index("pcol")
    x, z = grid_row // NZ, grid_row % NZ
    held_row = functools.reduce(jnp.logical_or, [z == i for i in range(NZ) if HELD_ROW[i]]).astype(jnp.int32)

    def plan(u):
        col = grid_col + u * COLS_GRID
        use0 = (pattern[0, col] != 0) & (col > 0)
        use1 = (pattern[1, col] != 0) & (col > 1)
        return use0, use1, use0 | use1 | (col < 2)

    def store(u):
        return pltpu.make_async_copy(work.at[u], out_hbm.at[:, u], out_sem.at[u])

    def passed(u):
        return [pltpu.make_async_copy(rows[t].at[u], out_hbm.at[t, u], out_sem.at[u]) for t in range(LR)]

    rows_of = pltpu.make_async_copy(pattern_hbm.at[0:8], pattern, sem)
    rows_of.start()
    operands = [
        pltpu.make_async_copy(mine_ref, lower.at[grid_col % 2], lower_sem.at[0]),
        pltpu.make_async_copy(neighbour_ref, lower.at[1 - grid_col % 2], lower_sem.at[1]),
    ]
    for k, refs in ((held_row, (held0, held1, held2, held3)), (1 - held_row, [pair.at[i] for pair in (other01, other23) for i in range(2)])):
        for shift, ref in enumerate(refs):
            part = pl.ds(pl.multiple_of((x + NX - shift) % NX * PIECE, PIECE), PIECE)
            operands.append(pltpu.make_async_copy(ref, upper.at[k, :, part, :], upper_sem.at[len(operands)]))
    for copy in operands:
        copy.start()
    rows_of.wait()

    def start_passed(u, carry):
        @pl.when(jnp.logical_not(plan(u)[2]))
        def _():
            for copy in passed(u):
                copy.start()

        return carry

    lax.fori_loop(0, LC, start_passed, 0)
    for copy in operands:
        copy.wait()

    def step(u, slots):
        use0, use1, touched = plan(u)
        slot0, slot1 = slots

        @pl.when(touched)
        def _():
            for t in range(LR):
                work[u, t] = rows[t][u]

            def update(k, slot):
                product = dot(lower[k].reshape(LR * B, B), upper[k, slot]).reshape(LR, B, B)
                work[u] = (work[u].astype(F32) - product).astype(BF16)

            @pl.when(use0)
            def _():
                update(0, slot0)

            @pl.when(use1)
            def _():
                update(1, slot1)

            for k in range(2):

                @pl.when((u == 0) & (grid_col == k))
                def _(k=k):
                    for t in range(LR):

                        @pl.when(t * ROWS_GRID + grid_row > k)
                        def _(t=t):
                            work[0, t] = lower[k, t]

            store(u).start()

        return slot0 + use0.astype(jnp.int32), slot1 + use1.astype(jnp.int32)

    lax.fori_loop(0, LC, step, (jnp.int32(0), jnp.int32(0)))

    def finish(u, carry):
        store(u).wait()
        return carry

    lax.fori_loop(0, LC, finish, 0)


def pick_by(index, options):
    value = None
    for i, option in enumerate(options):
        if option is not None:
            value = option if value is None else jnp.where(index == i, option, value)
    return value


def on_cols(rows, cols):
    return [(a * COLS_GRID + c, b * COLS_GRID + c) for a, b in rows for c in cols]


def along_z(pairs):
    return [(x * NZ + a, x * NZ + b) for x in range(NX) for a, b in pairs]


def scattered(sent):
    return [sent[0]] + [lax.ppermute(sent[d], "prow", [(z, d * NZ + z) for z in range(2)]) for d in range(1, NX)]


def select(part, table, *options, after=()):
    return pl.pallas_call(
        functools.partial(select_kernel, (part, tuple(table))),
        out_shape=jax.ShapeDtypeStruct(options[0].shape, options[0].dtype),
        in_specs=[vmem()] * len(options) + [anywhere()] * len(after),
        out_specs=vmem(),
        compiler_params=params(8),
        cost_estimate=cost(0, SELECT_BYTES),
        name="select",
    )(*options, *after)


def whole_pairs(z_pairs):
    rows = [[(x * NZ + a, x * NZ + b) for x in range(NX) for a, b in pairs] for pairs in z_pairs]
    return on_cols(rows[0], (0, 1)) + on_cols(rows[1], (1,))


def spread_whole(first, x, after):
    axes = ("prow", "pcol")
    starts = [on_cols([(0, d * NZ)], (0, 1)) + on_cols([(1, d * NZ + 1)], (1,)) for d in range(1, NX)]
    mine = pick_by(x, [first] + [lax.ppermute(first, axes, pairs) for pairs in starts])
    far_up, far_down = (lax.ppermute(mine, axes, whole_pairs(p)) for p in (FAR_UP, FAR_DOWN))
    held = select("z", (0, 0, 0, 1, 1, 2, 2, 0), mine, far_up, far_down, after=after)
    up, down = (lax.ppermute(held, axes, whole_pairs(p)) for p in (NEAR_UP, NEAR_DOWN))
    return held, up, down


def gather_x(own):
    shifted = [[(r, (r + d * NZ) % ROWS_GRID) for r in range(ROWS_GRID)] for d in range(1, NX)]
    return [own] + [lax.ppermute(own, "prow", pairs) for pairs in shifted]


def vmem():
    return pl.BlockSpec(memory_space=pltpu.VMEM)


def hbm():
    return pl.BlockSpec(memory_space=pltpu.HBM)


def in_hbm(value):
    return pltpu.with_memory_space_constraint(value, pltpu.HBM)


def anywhere():
    return pl.BlockSpec(memory_space=pl.ANY)


def like(*shape):
    return jax.ShapeDtypeStruct(shape, BF16)


def params(limit):
    return pltpu.CompilerParams(vmem_limit_bytes=limit * MIB)


def cost(flops, moved):
    return pl.CostEstimate(flops=flops, bytes_accessed=moved, transcendentals=0)


def local(matrix, row_perm, block_pattern):
    grid_row = lax.axis_index("prow")
    grid_col = lax.axis_index("pcol")
    x, z = grid_row // NZ, grid_row % NZ
    blocks = in_hbm(jnp.transpose(matrix[0, :, :, 0], (0, 2, 1, 3)))
    orders = in_hbm(row_perm.reshape(LR, 1, B))
    block_pattern = in_hbm(block_pattern)
    block = B * B * 2
    small_scratch = [pltpu.SMEM((8, NB), jnp.int32), pltpu.VMEM((1, B), jnp.int32)]
    dma = pltpu.SemaphoreType.DMA

    def permute(t, after):
        return pl.pallas_call(
            functools.partial(permute_kernel, t),
            out_shape=pltpu.VMEM((LC, B, B), BF16),
            in_specs=[hbm()] * 3 + [anywhere()],
            out_specs=vmem(),
            scratch_shapes=small_scratch + [pltpu.VMEM((LC, B, B), BF16), dma((2,)), dma((LC,))],
            compiler_params=params(16),
            cost_estimate=cost(2 * LC * B**3, 2 * LC * block),
            name="permute",
        )(block_pattern, orders, blocks, after)

    packed, first = pl.pallas_call(
        pack_kernel,
        out_shape=(like(NX, UCAP, PIECE, B), like(B, B)),
        in_specs=[hbm(), hbm(), hbm()],
        out_specs=(vmem(), vmem()),
        scratch_shapes=small_scratch + [pltpu.VMEM((LC, B, B), BF16), dma((2,)), dma((LC,))],
        compiler_params=params(16),
        cost_estimate=cost(2 * 7 * B**3, 19 * block),
        name="pack",
    )(block_pattern, orders, blocks)

    mine = select("x", range(NX), *scattered([packed[d] for d in range(NX)]))
    held, up, down = spread_whole(first, x, (mine,))
    skipped = [lax.ppermute(mine, "prow", along_z(skip_z(skip))) for skip in SKIPS]
    placed = []
    held_row = select("z", SKIP_OF, mine, *skipped)
    held_rows = gather_x(held_row)
    other_rows = [
        lax.ppermute(jnp.stack(held_rows[i : i + 2]), "prow", along_z(ring_z(step))) for i, step in ((0, 1), (2, -1))
    ]

    lower0, first0, high, low, column = pl.pallas_call(
        inverse_kernel,
        out_shape=(like(LR, B, B), like(B, B), like(B, B), like(B, B), like(LR, B, B)),
        in_specs=[vmem(), vmem(), vmem(), hbm(), hbm(), hbm(), anywhere()],
        out_specs=(vmem(),) * 5,
        scratch_shapes=[
            pltpu.SMEM((LR, 8, NB), jnp.int32),
            pltpu.VMEM((LR, 1, B), jnp.int32),
            pltpu.VMEM((LR, B, B), BF16),
            dma((2,)),
            dma((LR,)),
        ],
        compiler_params=params(16),
        cost_estimate=cost(2 * 18 * B**3, 12 * block),
        name="inverse",
    )(held, up, down, block_pattern, orders, blocks, held_row)

    neighbour0 = lax.ppermute(lower0, "pcol", [(0, 1)])
    lower = pl.pallas_call(
        second_kernel,
        out_shape=like(LR, B, B),
        in_specs=[vmem()] * 6,
        out_specs=vmem(),
        compiler_params=params(16),
        cost_estimate=cost(2 * 9 * B**3, 12 * block),
        name="second",
    )(lower0, neighbour0, first0, high, low, column)

    placed += [permute(t, lower) for t in range(LR)]
    got = [lax.ppermute(lower, "pcol", [(0, 2 * d), (1, 2 * d + 1)]) for d in (3, 1, 2)]
    lower_mine = select("y", (0, 2, 3, 1), lower, *got, after=placed)
    lower_neighbour = lax.ppermute(lower_mine, "pcol", [(c, c ^ 1) for c in range(COLS_GRID)])

    current = pl.pallas_call(
        schur_kernel,
        out_shape=like(LR, LC, B, B),
        in_specs=[hbm()] + [anywhere()] * (NX + 4) + [vmem()] * LR,
        out_specs=hbm(),
        scratch_shapes=[
            pltpu.SMEM((8, NB), jnp.int32),
            pltpu.VMEM((2, UCAP, B, B), BF16),
            pltpu.VMEM((2, LR, B, B), BF16),
            pltpu.VMEM((LC, LR, B, B), BF16),
            dma,
            dma((2 * NX + 2,)),
            dma((2,)),
            dma((LC,)),
        ],
        compiler_params=params(24),
        cost_estimate=cost(2 * LR * 12 * B**3, 90 * block),
        name="schur",
    )(block_pattern, *held_rows, *other_rows, lower_mine, lower_neighbour, *placed)
    return jnp.transpose(current, (0, 2, 1, 3)).reshape(matrix.shape)


def solution(mesh):
    placed = (P("prow", None, None, "pcol", None, None), P("prow", None, None), P())
    return jax.shard_map(
        local,
        mesh=mesh,
        in_specs=placed,
        out_specs=P("prow", None, None, "pcol", None, None),
        check_vma=False,
    )
```

```python
import functools

import jax
import jax.numpy as jnp
from jax import lax
from jax.experimental import pallas as pl
from jax.experimental.pallas import tpu as pltpu
from jax.sharding import PartitionSpec as P

B = 256
LR = 3
LC = 12
NB = 96
UCAP = 6
NEWTON = 3
ROWS_GRID = 32
COLS_GRID = 8
NX = 4
NZ = 8
PIECE = B // NX
SELECT_BYTES = 8 << 20
MIB = 1 << 20

F32 = jnp.float32
BF16 = jnp.bfloat16

FAR_UP = ([(0, 3)], [(1, 4)])
FAR_DOWN = ([(0, 5)], [(1, 6)])
NEAR_UP = ([(0, 1), (3, 4), (5, 6)], [(1, 2), (4, 5), (6, 7)])
NEAR_DOWN = ([(0, 7), (3, 2)], [(1, 0), (4, 3)])
FROM_0 = "hudhuhud"
FROM_1 = "dhudhuhu"
SKIPS = (2, -2, 4)
SKIP_OF = (0, 0, 1, 1, 3, 3, 2, 2)
HELD_ROW = (0, 1) * (NZ // 2)


def skip_z(skip):
    return [(z, (z + skip) % NZ) for z in range(2)]


def ring_z(step):
    return [(z, (z + step) % NZ) for z in range(NZ)]


def one_hot_rows(order):
    source = lax.broadcasted_iota(jnp.int32, (B, B), 0)
    return jnp.where(source == order, 1.0, 0.0).T.astype(BF16)


def split(value, parts):
    out = []
    for _ in range(parts):
        head = value.astype(BF16)
        out.append(head)
        value = value - head.astype(F32)
    return out


def dot(a, b):
    return jnp.dot(a, b, preferred_element_type=F32)


def pack_kernel(pattern_hbm, order_hbm, blocks_hbm, packed_ref, first_ref, pattern, order, blocks, sem, block_sem):
    small = [
        pltpu.make_async_copy(order_hbm.at[0], order, sem.at[0]),
        pltpu.make_async_copy(pattern_hbm.at[0:8], pattern, sem.at[1]),
    ]
    fetches = [pltpu.make_async_copy(blocks_hbm.at[0, u], blocks.at[u], block_sem.at[u]) for u in range(LC)]
    for copy in small + fetches:
        copy.start()
    for copy in small:
        copy.wait()
    supernode = jnp.minimum(lax.axis_index("prow"), 1)
    grid_col = lax.axis_index("pcol")
    pick = one_hot_rows(order[...])
    slot = jnp.int32(0)
    chosen = [jnp.int32(0)] * UCAP
    for u in range(LC):
        col = grid_col + u * COLS_GRID
        used = (pattern[supernode, col] != 0) & (col > supernode)
        chosen = [jnp.where(used & (slot == s), u, c) for s, c in enumerate(chosen)]
        slot = slot + used.astype(jnp.int32)
    for copy in fetches:
        copy.wait()
    present = pattern[supernode, grid_col] != 0
    first_ref[...] = jnp.where(present, dot(pick, blocks[0]), 0.0).astype(BF16)
    for s, u in enumerate(chosen):
        block = dot(pick, blocks[u]).astype(BF16)
        for piece in range(NX):
            packed_ref[piece, s] = block[piece * PIECE : (piece + 1) * PIECE]


def permute_kernel(
    pattern_hbm, order_hbm, blocks_hbm, after, placed_ref, out_hbm, pattern, orders, blocks, sem, pattern_sem, block_sem, out_sem
):
    del after
    grid_row = lax.axis_index("prow")
    grid_col = lax.axis_index("pcol")
    small = [pltpu.make_async_copy(order_hbm, orders, sem)]
    for t in range(LR):
        group = pl.ds(pl.multiple_of((t * ROWS_GRID + grid_row) // 8 * 8, 8), 8)
        small.append(pltpu.make_async_copy(pattern_hbm.at[group], pattern.at[t], pattern_sem.at[t]))

    def fetch(t):
        return pltpu.make_async_copy(blocks_hbm.at[t], blocks.at[t], block_sem.at[t])

    def store(t):
        return pltpu.make_async_copy(placed_ref.at[t], out_hbm.at[t], out_sem.at[t])

    for copy in small:
        copy.start()
    for t in range(LR):
        fetch(t).start()
    for copy in small:
        copy.wait()

    def block_row(t, carry):
        pick = one_hot_rows(orders[t])
        fetch(t).wait()
        for u in range(LC):
            present = pattern[t, grid_row % 8, grid_col + u * COLS_GRID] != 0
            placed_ref[t, u] = jnp.where(present, dot(pick, blocks[t, u]), 0.0).astype(BF16)
        store(t).start()
        return carry

    lax.fori_loop(0, LR, block_row, 0)
    for t in range(LR):
        store(t).wait()


def select_kernel(choices, *refs):
    *options, out_ref = refs
    part, table = choices
    grid_row = lax.axis_index("prow")
    place = {"x": grid_row // NZ, "z": grid_row % NZ, "y": lax.axis_index("pcol") // 2}[part]
    for i in range(max(table) + 1):
        hit = functools.reduce(jnp.logical_or, [place == p for p, choice in enumerate(table) if choice == i])

        @pl.when(hit)
        def _(i=i):
            out_ref[...] = options[i][...]


def inverse_kernel(
    held_ref, up_ref, down_ref, pattern_hbm, order_hbm, blocks_hbm, after,
    lower_ref, first_ref, high_ref, low_ref, column_ref,
    pattern, orders, blocks, sem, pattern_sem,
):
    del after
    grid_row = lax.axis_index("prow")
    grid_col = lax.axis_index("pcol")
    z = grid_row % NZ

    def chosen(table):
        def of(letter, ref):
            hit = functools.reduce(jnp.logical_or, [z == i for i in range(NZ) if table[i] == letter])
            return hit, ref

        (held, h), (up, u) = of("h", held_ref), of("u", up_ref)
        return jnp.where(
            held, h[...].astype(F32), jnp.where(up, u[...].astype(F32), down_ref[...].astype(F32))
        )

    @pl.when(grid_col < 2)
    def _():
        fetches = [
            pltpu.make_async_copy(order_hbm, orders, sem.at[0]),
            pltpu.make_async_copy(blocks_hbm.at[:, 0], blocks, sem.at[1]),
        ]
        for t in range(LR):
            group = pl.ds(pl.multiple_of((t * ROWS_GRID + grid_row) // 8 * 8, 8), 8)
            fetches.append(pltpu.make_async_copy(pattern_hbm.at[group], pattern.at[t], pattern_sem.at[t]))
        for copy in fetches:
            copy.start()
        first = chosen(FROM_0)
        first_ref[...] = first.astype(BF16)
        block = jnp.where(grid_col == 0, first, chosen(FROM_1))
        diagonal = lax.broadcasted_iota(jnp.int32, (B, B), 0) == lax.broadcasted_iota(jnp.int32, (B, B), 1)
        pivots = jnp.where(diagonal, block, 0.0)
        by_col = 1.0 / jnp.sum(pivots, axis=0, keepdims=True)
        by_row = 1.0 / jnp.sum(pivots, axis=1, keepdims=True)
        twice = jnp.where(diagonal, 2.0, 0.0)
        inverse = by_row * (twice - block * by_col)
        block16 = block.astype(BF16)
        for _ in range(NEWTON - 1):
            high, middle, low = split(inverse, 3)
            rest = twice - (dot(block16, high) + (dot(block16, middle) + dot(block16, low)))
            rest_high, rest_low = split(rest, 2)
            inverse = dot(high, rest_high) + (dot(high, rest_low) + dot(middle, rest_high))
        high, low = split(inverse, 2)
        high_ref[...] = high
        low_ref[...] = low
        for copy in fetches:
            copy.wait()
        for t in range(LR):
            present = pattern[t, grid_row % 8, grid_col] != 0
            column = jnp.where(present, dot(one_hot_rows(orders[t]), blocks[t]), 0.0).astype(BF16)
            column_ref[t] = column
            lower = dot(column, high) + dot(column, low)
            lower_ref[t] = jnp.where(t * ROWS_GRID + grid_row > 0, lower, 0.0).astype(BF16)


def second_kernel(own_ref, lower_ref, first_ref, high_ref, low_ref, column_ref, out_ref):
    grid_row = lax.axis_index("prow")

    @pl.when(lax.axis_index("pcol") == 0)
    def _():
        out_ref[...] = own_ref[...]

    @pl.when(lax.axis_index("pcol") == 1)
    def _():
        for t in range(LR):
            rest = (column_ref[t].astype(F32) - dot(lower_ref[t], first_ref[...])).astype(BF16)
            lower = dot(rest, high_ref[...]) + dot(rest, low_ref[...])
            out_ref[t] = jnp.where(t * ROWS_GRID + grid_row > 1, lower, 0.0).astype(BF16)


def schur_kernel(
    pattern_hbm, held0, held1, held2, held3, other01, other23, mine_ref, neighbour_ref, placed, current_hbm,
    out_hbm, pattern, upper, work, sem, upper_sem, out_sem,
):
    del current_hbm
    grid_row = lax.axis_index("prow")
    grid_col = lax.axis_index("pcol")
    x, z = grid_row // NZ, grid_row % NZ
    held_row = functools.reduce(jnp.logical_or, [z == i for i in range(NZ) if HELD_ROW[i]]).astype(jnp.int32)

    def plan(u):
        col = grid_col + u * COLS_GRID
        use0 = (pattern[0, col] != 0) & (col > 0)
        use1 = (pattern[1, col] != 0) & (col > 1)
        return use0, use1, use0 | use1 | (col < 2)

    def store(u):
        return pltpu.make_async_copy(work.at[u], out_hbm.at[:, u], out_sem.at[u])

    rows_of = pltpu.make_async_copy(pattern_hbm.at[0:8], pattern, sem)
    rows_of.start()
    operands = []
    for k, refs in ((held_row, (held0, held1, held2, held3)), (1 - held_row, [pair.at[i] for pair in (other01, other23) for i in range(2)])):
        for shift, ref in enumerate(refs):
            part = pl.ds(pl.multiple_of((x + NX - shift) % NX * PIECE, PIECE), PIECE)
            operands.append(pltpu.make_async_copy(ref, upper.at[k, :, part, :], upper_sem.at[len(operands)]))
    for copy in operands:
        copy.start()
    rows_of.wait()

    for copy in operands:
        copy.wait()

    def step(u, slots):
        use0, use1, touched = plan(u)
        slot0, slot1 = slots

        @pl.when(touched)
        def _():
            @pl.when(jnp.logical_not(use0))
            def _():
                for t in range(LR):
                    work[u, t] = placed[t, u]

            for k, used, slot in ((0, use0, slot0), (1, use1, slot1)):
                for parity, lower in ((k, mine_ref), (1 - k, neighbour_ref)):

                    @pl.when(used & (grid_col % 2 == parity))
                    def _(k=k, slot=slot, lower=lower):
                        for t in range(LR):
                            block = work[u, t] if k else placed[t, u]
                            work[u, t] = (block.astype(F32) - dot(lower[t], upper[k, slot])).astype(BF16)

            @pl.when((u == 0) & (grid_col < 2))
            def _():
                for t in range(LR):

                    @pl.when(t * ROWS_GRID + grid_row > grid_col)
                    def _(t=t):
                        work[0, t] = mine_ref[t]

            store(u).start()

        return slot0 + use0.astype(jnp.int32), slot1 + use1.astype(jnp.int32)

    lax.fori_loop(0, LC, step, (jnp.int32(0), jnp.int32(0)))

    def finish(u, carry):
        @pl.when(plan(u)[2])
        def _():
            store(u).wait()

        return carry

    lax.fori_loop(0, LC, finish, 0)


def pick_by(index, options):
    value = None
    for i, option in enumerate(options):
        if option is not None:
            value = option if value is None else jnp.where(index == i, option, value)
    return value


def on_cols(rows, cols):
    return [(a * COLS_GRID + c, b * COLS_GRID + c) for a, b in rows for c in cols]


def along_z(pairs):
    return [(x * NZ + a, x * NZ + b) for x in range(NX) for a, b in pairs]


def scattered(sent):
    return [sent[0]] + [lax.ppermute(sent[d], "prow", [(z, d * NZ + z) for z in range(2)]) for d in range(1, NX)]


def select(part, table, *options, after=()):
    return pl.pallas_call(
        functools.partial(select_kernel, (part, tuple(table))),
        out_shape=jax.ShapeDtypeStruct(options[0].shape, options[0].dtype),
        in_specs=[vmem()] * len(options) + [anywhere()] * len(after),
        out_specs=vmem(),
        compiler_params=params(8),
        cost_estimate=cost(0, SELECT_BYTES),
        name="select",
    )(*options, *after)


def whole_pairs(z_pairs):
    rows = [[(x * NZ + a, x * NZ + b) for x in range(NX) for a, b in pairs] for pairs in z_pairs]
    return on_cols(rows[0], (0, 1)) + on_cols(rows[1], (1,))


def spread_whole(first, x, after):
    axes = ("prow", "pcol")
    starts = [on_cols([(0, d * NZ)], (0, 1)) + on_cols([(1, d * NZ + 1)], (1,)) for d in range(1, NX)]
    mine = pick_by(x, [first] + [lax.ppermute(first, axes, pairs) for pairs in starts])
    far_up, far_down = (lax.ppermute(mine, axes, whole_pairs(p)) for p in (FAR_UP, FAR_DOWN))
    held = select("z", (0, 0, 0, 1, 1, 2, 2, 0), mine, far_up, far_down, after=after)
    up, down = (lax.ppermute(held, axes, whole_pairs(p)) for p in (NEAR_UP, NEAR_DOWN))
    return held, up, down


def gather_x(own):
    shifted = [[(r, (r + d * NZ) % ROWS_GRID) for r in range(ROWS_GRID)] for d in range(1, NX)]
    return [own] + [lax.ppermute(own, "prow", pairs) for pairs in shifted]


def vmem():
    return pl.BlockSpec(memory_space=pltpu.VMEM)


def hbm():
    return pl.BlockSpec(memory_space=pltpu.HBM)


def in_hbm(value):
    return pltpu.with_memory_space_constraint(value, pltpu.HBM)


def anywhere():
    return pl.BlockSpec(memory_space=pl.ANY)


def like(*shape):
    return jax.ShapeDtypeStruct(shape, BF16)


def params(limit):
    return pltpu.CompilerParams(vmem_limit_bytes=limit * MIB)


def cost(flops, moved):
    return pl.CostEstimate(flops=flops, bytes_accessed=moved, transcendentals=0)


def local(matrix, row_perm, block_pattern):
    grid_row = lax.axis_index("prow")
    grid_col = lax.axis_index("pcol")
    x, z = grid_row // NZ, grid_row % NZ
    blocks = in_hbm(jnp.transpose(matrix[0, :, :, 0], (0, 2, 1, 3)))
    orders = in_hbm(row_perm.reshape(LR, 1, B))
    block_pattern = in_hbm(block_pattern)
    block = B * B * 2
    small_scratch = [pltpu.SMEM((8, NB), jnp.int32), pltpu.VMEM((1, B), jnp.int32)]
    dma = pltpu.SemaphoreType.DMA

    packed, first = pl.pallas_call(
        pack_kernel,
        out_shape=(like(NX, UCAP, PIECE, B), like(B, B)),
        in_specs=[hbm(), hbm(), hbm()],
        out_specs=(vmem(), vmem()),
        scratch_shapes=small_scratch + [pltpu.VMEM((LC, B, B), BF16), dma((2,)), dma((LC,))],
        compiler_params=params(16),
        cost_estimate=cost(2 * 7 * B**3, 19 * block),
        name="pack",
    )(block_pattern, orders, blocks)

    mine = select("x", range(NX), *scattered([packed[d] for d in range(NX)]))
    held, up, down = spread_whole(first, x, (mine,))
    skipped = [lax.ppermute(mine, "prow", along_z(skip_z(skip))) for skip in SKIPS]
    held_row = select("z", SKIP_OF, mine, *skipped)
    held_rows = gather_x(held_row)
    other_rows = [
        lax.ppermute(jnp.stack(held_rows[i : i + 2]), "prow", along_z(ring_z(step))) for i, step in ((0, 1), (2, -1))
    ]

    lower0, first0, high, low, column = pl.pallas_call(
        inverse_kernel,
        out_shape=(like(LR, B, B), like(B, B), like(B, B), like(B, B), like(LR, B, B)),
        in_specs=[vmem(), vmem(), vmem(), hbm(), hbm(), hbm(), anywhere()],
        out_specs=(vmem(),) * 5,
        scratch_shapes=[
            pltpu.SMEM((LR, 8, NB), jnp.int32),
            pltpu.VMEM((LR, 1, B), jnp.int32),
            pltpu.VMEM((LR, B, B), BF16),
            dma((2,)),
            dma((LR,)),
        ],
        compiler_params=params(16),
        cost_estimate=cost(2 * 18 * B**3, 12 * block),
        name="inverse",
    )(held, up, down, block_pattern, orders, blocks, held_row)

    neighbour0 = lax.ppermute(lower0, "pcol", [(0, 1)])
    lower = pl.pallas_call(
        second_kernel,
        out_shape=like(LR, B, B),
        in_specs=[vmem()] * 6,
        out_specs=vmem(),
        compiler_params=params(16),
        cost_estimate=cost(2 * 9 * B**3, 12 * block),
        name="second",
    )(lower0, neighbour0, first0, high, low, column)

    placed, current = pl.pallas_call(
        permute_kernel,
        out_shape=(pltpu.VMEM((LR, LC, B, B), BF16), like(LR, LC, B, B)),
        in_specs=[hbm()] * 3 + [anywhere()],
        out_specs=(vmem(), hbm()),
        scratch_shapes=[
            pltpu.SMEM((LR, 8, NB), jnp.int32),
            pltpu.VMEM((LR, 1, B), jnp.int32),
            pltpu.VMEM((LR, LC, B, B), BF16),
            dma,
            dma((LR,)),
            dma((LR,)),
            dma((LR,)),
        ],
        compiler_params=params(16),
        cost_estimate=cost(2 * LR * LC * B**3, 2 * LR * LC * block),
        name="permute",
    )(block_pattern, orders, blocks, lower)
    got = [lax.ppermute(lower, "pcol", [(0, 2 * d), (1, 2 * d + 1)]) for d in (3, 1, 2)]
    lower_mine = select("y", (0, 2, 3, 1), lower, *got, after=(placed,))
    lower_neighbour = lax.ppermute(lower_mine, "pcol", [(c, c ^ 1) for c in range(COLS_GRID)])

    current = pl.pallas_call(
        schur_kernel,
        out_shape=like(LR, LC, B, B),
        in_specs=[hbm()] + [anywhere()] * (NX + 2) + [vmem()] * 3 + [hbm()],
        out_specs=hbm(),
        scratch_shapes=[
            pltpu.SMEM((8, NB), jnp.int32),
            pltpu.VMEM((2, UCAP, B, B), BF16),
            pltpu.VMEM((LC, LR, B, B), BF16),
            dma,
            dma((2 * NX,)),
            dma((LC,)),
        ],
        input_output_aliases={NX + 6: 0},
        compiler_params=params(24),
        cost_estimate=cost(2 * LR * 12 * B**3, 90 * block),
        name="schur",
    )(block_pattern, *held_rows, *other_rows, lower_mine, lower_neighbour, placed, current)
    return jnp.transpose(current, (0, 2, 1, 3)).reshape(matrix.shape)


def solution(mesh):
    placed = (P("prow", None, None, "pcol", None, None), P("prow", None, None), P())
    return jax.shard_map(
        local,
        mesh=mesh,
        in_specs=placed,
        out_specs=P("prow", None, None, "pcol", None, None),
        check_vma=False,
    )
```

```python
import functools

import jax
import jax.numpy as jnp
from jax import lax
from jax.experimental import pallas as pl
from jax.experimental.pallas import tpu as pltpu
from jax.sharding import PartitionSpec as P

B = 256
LR = 3
LC = 12
NB = 96
UCAP = 6
NEWTON = 3
ROWS_GRID = 32
COLS_GRID = 8
NX = 4
NZ = 8
PIECE = B // NX
SELECT_BYTES = 8 << 20
MIB = 1 << 20

F32 = jnp.float32
BF16 = jnp.bfloat16

FAR_UP = ([(0, 3)], [(1, 4)])
FAR_DOWN = ([(0, 5)], [(1, 6)])
NEAR_UP = ([(0, 1), (3, 4), (5, 6)], [(1, 2), (4, 5), (6, 7)])
NEAR_DOWN = ([(0, 7), (3, 2)], [(1, 0), (4, 3)])
FROM_0 = "hudhuhud"
FROM_1 = "dhudhuhu"
SKIPS = (2, -2, 4)
SKIP_OF = (0, 0, 1, 1, 3, 3, 2, 2)
HELD_ROW = (0, 1) * (NZ // 2)


def skip_z(skip):
    return [(z, (z + skip) % NZ) for z in range(2)]


def ring_z(step):
    return [(z, (z + step) % NZ) for z in range(NZ)]


def one_hot_rows(order):
    source = lax.broadcasted_iota(jnp.int32, (B, B), 0)
    return jnp.where(source == order, 1.0, 0.0).T.astype(BF16)


def split(value, parts):
    out = []
    for _ in range(parts):
        head = value.astype(BF16)
        out.append(head)
        value = value - head.astype(F32)
    return out


def dot(a, b):
    return jnp.dot(a, b, preferred_element_type=F32)


def pack_kernel(pattern_hbm, order_hbm, blocks_hbm, packed_ref, first_ref, pattern, order, blocks, sem, block_sem):
    small = [
        pltpu.make_async_copy(order_hbm.at[0], order, sem.at[0]),
        pltpu.make_async_copy(pattern_hbm.at[0:8], pattern, sem.at[1]),
    ]
    fetches = [pltpu.make_async_copy(blocks_hbm.at[0, u], blocks.at[u], block_sem.at[u]) for u in range(LC)]
    for copy in small + fetches:
        copy.start()
    for copy in small:
        copy.wait()
    supernode = jnp.minimum(lax.axis_index("prow"), 1)
    grid_col = lax.axis_index("pcol")
    pick = one_hot_rows(order[...])
    slot = jnp.int32(0)
    chosen = [jnp.int32(0)] * UCAP
    for u in range(LC):
        col = grid_col + u * COLS_GRID
        used = (pattern[supernode, col] != 0) & (col > supernode)
        chosen = [jnp.where(used & (slot == s), u, c) for s, c in enumerate(chosen)]
        slot = slot + used.astype(jnp.int32)
    for copy in fetches:
        copy.wait()
    present = pattern[supernode, grid_col] != 0
    first_ref[...] = jnp.where(present, dot(pick, blocks[0]), 0.0).astype(BF16)
    for s, u in enumerate(chosen):
        block = dot(pick, blocks[u]).astype(BF16)
        for piece in range(NX):
            packed_ref[piece, s] = block[piece * PIECE : (piece + 1) * PIECE]


def permute_kernel(
    pattern_hbm, order_hbm, blocks_hbm, after, placed_ref, pattern, orders, blocks, sem, pattern_sem, block_sem
):
    del after
    grid_row = lax.axis_index("prow")
    grid_col = lax.axis_index("pcol")
    small = [pltpu.make_async_copy(order_hbm, orders, sem)]
    for t in range(LR):
        group = pl.ds(pl.multiple_of((t * ROWS_GRID + grid_row) // 8 * 8, 8), 8)
        small.append(pltpu.make_async_copy(pattern_hbm.at[group], pattern.at[t], pattern_sem.at[t]))

    def fetch(t):
        return pltpu.make_async_copy(blocks_hbm.at[t], blocks.at[t], block_sem.at[t])

    for copy in small:
        copy.start()
    for t in range(LR):
        fetch(t).start()
    for copy in small:
        copy.wait()

    def block_row(t, carry):
        pick = one_hot_rows(orders[t])
        fetch(t).wait()
        for u in range(LC):
            present = pattern[t, grid_row % 8, grid_col + u * COLS_GRID] != 0
            placed_ref[t, u] = jnp.where(present, dot(pick, blocks[t, u]), 0.0).astype(BF16)
        return carry

    lax.fori_loop(0, LR, block_row, 0)


def select_kernel(choices, *refs):
    *options, out_ref = refs
    part, table = choices
    grid_row = lax.axis_index("prow")
    place = {"x": grid_row // NZ, "z": grid_row % NZ, "y": lax.axis_index("pcol") // 2}[part]
    for i in range(max(table) + 1):
        hit = functools.reduce(jnp.logical_or, [place == p for p, choice in enumerate(table) if choice == i])

        @pl.when(hit)
        def _(i=i):
            out_ref[...] = options[i][...]


def inverse_kernel(
    held_ref, up_ref, down_ref, pattern_hbm, order_hbm, blocks_hbm, after,
    lower_ref, first_ref, high_ref, low_ref, column_ref,
    pattern, orders, blocks, sem, pattern_sem,
):
    del after
    grid_row = lax.axis_index("prow")
    grid_col = lax.axis_index("pcol")
    z = grid_row % NZ

    def chosen(table):
        def of(letter, ref):
            hit = functools.reduce(jnp.logical_or, [z == i for i in range(NZ) if table[i] == letter])
            return hit, ref

        (held, h), (up, u) = of("h", held_ref), of("u", up_ref)
        return jnp.where(
            held, h[...].astype(F32), jnp.where(up, u[...].astype(F32), down_ref[...].astype(F32))
        )

    @pl.when(grid_col < 2)
    def _():
        fetches = [
            pltpu.make_async_copy(order_hbm, orders, sem.at[0]),
            pltpu.make_async_copy(blocks_hbm.at[:, 0], blocks, sem.at[1]),
        ]
        for t in range(LR):
            group = pl.ds(pl.multiple_of((t * ROWS_GRID + grid_row) // 8 * 8, 8), 8)
            fetches.append(pltpu.make_async_copy(pattern_hbm.at[group], pattern.at[t], pattern_sem.at[t]))
        for copy in fetches:
            copy.start()
        first = chosen(FROM_0)
        first_ref[...] = first.astype(BF16)
        block = jnp.where(grid_col == 0, first, chosen(FROM_1))
        diagonal = lax.broadcasted_iota(jnp.int32, (B, B), 0) == lax.broadcasted_iota(jnp.int32, (B, B), 1)
        pivots = jnp.where(diagonal, block, 0.0)
        by_col = 1.0 / jnp.sum(pivots, axis=0, keepdims=True)
        by_row = 1.0 / jnp.sum(pivots, axis=1, keepdims=True)
        twice = jnp.where(diagonal, 2.0, 0.0)
        inverse = by_row * (twice - block * by_col)
        block16 = block.astype(BF16)
        for _ in range(NEWTON - 1):
            high, middle, low = split(inverse, 3)
            rest = twice - (dot(block16, high) + (dot(block16, middle) + dot(block16, low)))
            rest_high, rest_low = split(rest, 2)
            inverse = dot(high, rest_high) + (dot(high, rest_low) + dot(middle, rest_high))
        high, low = split(inverse, 2)
        high_ref[...] = high
        low_ref[...] = low
        for copy in fetches:
            copy.wait()
        for t in range(LR):
            present = pattern[t, grid_row % 8, grid_col] != 0
            column = jnp.where(present, dot(one_hot_rows(orders[t]), blocks[t]), 0.0).astype(BF16)
            column_ref[t] = column
            lower = dot(column, high) + dot(column, low)
            lower_ref[t] = jnp.where(t * ROWS_GRID + grid_row > 0, lower, 0.0).astype(BF16)


def second_kernel(own_ref, lower_ref, first_ref, high_ref, low_ref, column_ref, out_ref):
    grid_row = lax.axis_index("prow")

    @pl.when(lax.axis_index("pcol") == 0)
    def _():
        out_ref[...] = own_ref[...]

    @pl.when(lax.axis_index("pcol") == 1)
    def _():
        for t in range(LR):
            rest = (column_ref[t].astype(F32) - dot(lower_ref[t], first_ref[...])).astype(BF16)
            lower = dot(rest, high_ref[...]) + dot(rest, low_ref[...])
            out_ref[t] = jnp.where(t * ROWS_GRID + grid_row > 1, lower, 0.0).astype(BF16)


def schur_kernel(
    pattern_hbm, held0, held1, held2, held3, other01, other23, mine_ref, neighbour_ref, placed,
    out_hbm, pattern, upper, work, sem, upper_sem, out_sem,
):
    grid_row = lax.axis_index("prow")
    grid_col = lax.axis_index("pcol")
    x, z = grid_row // NZ, grid_row % NZ
    held_row = functools.reduce(jnp.logical_or, [z == i for i in range(NZ) if HELD_ROW[i]]).astype(jnp.int32)

    def plan(u):
        col = grid_col + u * COLS_GRID
        use0 = (pattern[0, col] != 0) & (col > 0)
        use1 = (pattern[1, col] != 0) & (col > 1)
        return use0, use1, use0 | use1 | (col < 2)

    def store(u):
        return pltpu.make_async_copy(work.at[u], out_hbm.at[:, u], out_sem.at[u])

    def passed(u):
        return pltpu.make_async_copy(placed.at[:, u], out_hbm.at[:, u], out_sem.at[u])

    rows_of = pltpu.make_async_copy(pattern_hbm.at[0:8], pattern, sem)
    rows_of.start()
    operands = []
    for k, refs in ((held_row, (held0, held1, held2, held3)), (1 - held_row, [pair.at[i] for pair in (other01, other23) for i in range(2)])):
        for shift, ref in enumerate(refs):
            part = pl.ds(pl.multiple_of((x + NX - shift) % NX * PIECE, PIECE), PIECE)
            operands.append(pltpu.make_async_copy(ref, upper.at[k, :, part, :], upper_sem.at[len(operands)]))
    for copy in operands:
        copy.start()
    rows_of.wait()

    def start_passed(u, carry):
        @pl.when(jnp.logical_not(plan(u)[2]))
        def _():
            passed(u).start()

        return carry

    lax.fori_loop(0, LC, start_passed, 0)
    for copy in operands:
        copy.wait()

    def step(u, slots):
        use0, use1, touched = plan(u)
        slot0, slot1 = slots

        @pl.when(touched)
        def _():
            @pl.when(jnp.logical_not(use0))
            def _():
                for t in range(LR):
                    work[u, t] = placed[t, u]

            for k, used, slot in ((0, use0, slot0), (1, use1, slot1)):
                for parity, lower in ((k, mine_ref), (1 - k, neighbour_ref)):

                    @pl.when(used & (grid_col % 2 == parity))
                    def _(k=k, slot=slot, lower=lower):
                        for t in range(LR):
                            block = work[u, t] if k else placed[t, u]
                            work[u, t] = (block.astype(F32) - dot(lower[t], upper[k, slot])).astype(BF16)

            @pl.when((u == 0) & (grid_col < 2))
            def _():
                for t in range(LR):

                    @pl.when(t * ROWS_GRID + grid_row > grid_col)
                    def _(t=t):
                        work[0, t] = mine_ref[t]

            store(u).start()

        return slot0 + use0.astype(jnp.int32), slot1 + use1.astype(jnp.int32)

    lax.fori_loop(0, LC, step, (jnp.int32(0), jnp.int32(0)))

    def finish(u, carry):
        store(u).wait()
        return carry

    lax.fori_loop(0, LC, finish, 0)


def pick_by(index, options):
    value = None
    for i, option in enumerate(options):
        if option is not None:
            value = option if value is None else jnp.where(index == i, option, value)
    return value


def on_cols(rows, cols):
    return [(a * COLS_GRID + c, b * COLS_GRID + c) for a, b in rows for c in cols]


def along_z(pairs):
    return [(x * NZ + a, x * NZ + b) for x in range(NX) for a, b in pairs]


def scattered(sent):
    return [sent[0]] + [lax.ppermute(sent[d], "prow", [(z, d * NZ + z) for z in range(2)]) for d in range(1, NX)]


def select(part, table, *options, after=()):
    return pl.pallas_call(
        functools.partial(select_kernel, (part, tuple(table))),
        out_shape=jax.ShapeDtypeStruct(options[0].shape, options[0].dtype),
        in_specs=[vmem()] * len(options) + [anywhere()] * len(after),
        out_specs=vmem(),
        compiler_params=params(8),
        cost_estimate=cost(0, SELECT_BYTES),
        name="select",
    )(*options, *after)


def whole_pairs(z_pairs):
    rows = [[(x * NZ + a, x * NZ + b) for x in range(NX) for a, b in pairs] for pairs in z_pairs]
    return on_cols(rows[0], (0, 1)) + on_cols(rows[1], (1,))


def spread_whole(first, x, after):
    axes = ("prow", "pcol")
    starts = [on_cols([(0, d * NZ)], (0, 1)) + on_cols([(1, d * NZ + 1)], (1,)) for d in range(1, NX)]
    mine = pick_by(x, [first] + [lax.ppermute(first, axes, pairs) for pairs in starts])
    far_up, far_down = (lax.ppermute(mine, axes, whole_pairs(p)) for p in (FAR_UP, FAR_DOWN))
    held = select("z", (0, 0, 0, 1, 1, 2, 2, 0), mine, far_up, far_down, after=after)
    up, down = (lax.ppermute(held, axes, whole_pairs(p)) for p in (NEAR_UP, NEAR_DOWN))
    return held, up, down


def gather_x(own):
    shifted = [[(r, (r + d * NZ) % ROWS_GRID) for r in range(ROWS_GRID)] for d in range(1, NX)]
    return [own] + [lax.ppermute(own, "prow", pairs) for pairs in shifted]


def vmem():
    return pl.BlockSpec(memory_space=pltpu.VMEM)


def hbm():
    return pl.BlockSpec(memory_space=pltpu.HBM)


def in_hbm(value):
    return pltpu.with_memory_space_constraint(value, pltpu.HBM)


def anywhere():
    return pl.BlockSpec(memory_space=pl.ANY)


def like(*shape):
    return jax.ShapeDtypeStruct(shape, BF16)


def params(limit):
    return pltpu.CompilerParams(vmem_limit_bytes=limit * MIB)


def cost(flops, moved):
    return pl.CostEstimate(flops=flops, bytes_accessed=moved, transcendentals=0)


def local(matrix, row_perm, block_pattern):
    grid_row = lax.axis_index("prow")
    grid_col = lax.axis_index("pcol")
    x, z = grid_row // NZ, grid_row % NZ
    blocks = in_hbm(jnp.transpose(matrix[0, :, :, 0], (0, 2, 1, 3)))
    orders = in_hbm(row_perm.reshape(LR, 1, B))
    block_pattern = in_hbm(block_pattern)
    block = B * B * 2
    small_scratch = [pltpu.SMEM((8, NB), jnp.int32), pltpu.VMEM((1, B), jnp.int32)]
    dma = pltpu.SemaphoreType.DMA

    packed, first = pl.pallas_call(
        pack_kernel,
        out_shape=(like(NX, UCAP, PIECE, B), like(B, B)),
        in_specs=[hbm(), hbm(), hbm()],
        out_specs=(vmem(), vmem()),
        scratch_shapes=small_scratch + [pltpu.VMEM((LC, B, B), BF16), dma((2,)), dma((LC,))],
        compiler_params=params(16),
        cost_estimate=cost(2 * 7 * B**3, 19 * block),
        name="pack",
    )(block_pattern, orders, blocks)

    mine = select("x", range(NX), *scattered([packed[d] for d in range(NX)]))
    held, up, down = spread_whole(first, x, (mine,))
    skipped = [lax.ppermute(mine, "prow", along_z(skip_z(skip))) for skip in SKIPS]
    held_row = select("z", SKIP_OF, mine, *skipped)
    held_rows = gather_x(held_row)
    other_rows = [
        lax.ppermute(jnp.stack(held_rows[i : i + 2]), "prow", along_z(ring_z(step))) for i, step in ((0, 1), (2, -1))
    ]

    lower0, first0, high, low, column = pl.pallas_call(
        inverse_kernel,
        out_shape=(like(LR, B, B), like(B, B), like(B, B), like(B, B), like(LR, B, B)),
        in_specs=[vmem(), vmem(), vmem(), hbm(), hbm(), hbm(), anywhere()],
        out_specs=(vmem(),) * 5,
        scratch_shapes=[
            pltpu.SMEM((LR, 8, NB), jnp.int32),
            pltpu.VMEM((LR, 1, B), jnp.int32),
            pltpu.VMEM((LR, B, B), BF16),
            dma((2,)),
            dma((LR,)),
        ],
        compiler_params=params(16),
        cost_estimate=cost(2 * 18 * B**3, 12 * block),
        name="inverse",
    )(held, up, down, block_pattern, orders, blocks, held_row)

    neighbour0 = lax.ppermute(lower0, "pcol", [(0, 1)])
    lower = pl.pallas_call(
        second_kernel,
        out_shape=like(LR, B, B),
        in_specs=[vmem()] * 6,
        out_specs=vmem(),
        compiler_params=params(16),
        cost_estimate=cost(2 * 9 * B**3, 12 * block),
        name="second",
    )(lower0, neighbour0, first0, high, low, column)

    placed = pl.pallas_call(
        permute_kernel,
        out_shape=pltpu.VMEM((LR, LC, B, B), BF16),
        in_specs=[hbm()] * 3 + [anywhere()],
        out_specs=vmem(),
        scratch_shapes=[
            pltpu.SMEM((LR, 8, NB), jnp.int32),
            pltpu.VMEM((LR, 1, B), jnp.int32),
            pltpu.VMEM((LR, LC, B, B), BF16),
            dma,
            dma((LR,)),
            dma((LR,)),
        ],
        compiler_params=params(16),
        cost_estimate=cost(2 * LR * LC * B**3, 2 * LR * LC * block),
        name="permute",
    )(block_pattern, orders, blocks, lower)
    got = [lax.ppermute(lower, "pcol", [(0, 2 * d), (1, 2 * d + 1)]) for d in (3, 1, 2)]
    lower_mine = select("y", (0, 2, 3, 1), lower, *got, after=(placed,))
    lower_neighbour = lax.ppermute(lower_mine, "pcol", [(c, c ^ 1) for c in range(COLS_GRID)])

    current = pl.pallas_call(
        schur_kernel,
        out_shape=like(LR, LC, B, B),
        in_specs=[hbm()] + [anywhere()] * (NX + 2) + [vmem()] * 3,
        out_specs=hbm(),
        scratch_shapes=[
            pltpu.SMEM((8, NB), jnp.int32),
            pltpu.VMEM((2, UCAP, B, B), BF16),
            pltpu.VMEM((LC, LR, B, B), BF16),
            dma,
            dma((2 * NX,)),
            dma((LC,)),
        ],
        compiler_params=params(24),
        cost_estimate=cost(2 * LR * 12 * B**3, 90 * block),
        name="schur",
    )(block_pattern, *held_rows, *other_rows, lower_mine, lower_neighbour, placed)
    return jnp.transpose(current, (0, 2, 1, 3)).reshape(matrix.shape)


def solution(mesh):
    placed = (P("prow", None, None, "pcol", None, None), P("prow", None, None), P())
    return jax.shard_map(
        local,
        mesh=mesh,
        in_specs=placed,
        out_specs=P("prow", None, None, "pcol", None, None),
        check_vma=False,
    )
```
